512 devices in a mesh: dp: 64 (over x, z, core), tensor: 8 (over y).
Axes of the slice: x: 4, y: 8, z: 8, core: 2. Of those that a mesh axis runs over, the one named last changes fastest.
Arguments:
- queries: bfloat16 [32768, 4096], P('dp', 'tensor'), may hold values from -6 to 6
- keys: bfloat16 [32768, 1024], P('dp', 'tensor'), may hold values from -6 to 6
- values: bfloat16 [32768, 1024], P('dp', 'tensor'), may hold values from -6 to 6
- attn_out: bfloat16 [32768, 4096], P('dp', 'tensor'), may hold values from -6 to 6
- grad_out: bfloat16 [32768, 4096], P('dp', 'tensor'), may hold values from -24 to 24
- out_weight: bfloat16 [4096, 4096], P('dp', 'tensor'), may hold values from -0.09375 to 0.09375
- log_norm: float32 [32, 32768], P('tensor', 'dp')
- source_row: int32 [32768], P('dp'), may hold values from 0 to 32767, as said below
- dest_row: int32 [32768], P('dp'), may hold values from 0 to 32767, as said below
- slot_start: int32 [32768], P('dp'), may hold values from 0 to 32767, as said below
Outputs:
- grad_queries: bfloat16 [32768, 4096], P('dp', 'tensor')
- grad_keys: bfloat16 [32768, 1024], P('dp', 'tensor')
- grad_values: bfloat16 [32768, 1024], P('dp', 'tensor')
The draws below stay inside these ranges and needn't reach their ends.
Inputs may be any that keep to these rules, and one draw needn't show every extreme that they name: `source_row`: a permutation of the packed positions; every document lies whole and in order within one device's block of 512 tokens in both orders; a balanced slot of device i of dp holds a token of device i - 1, i or i + 1 in packed order; across every boundary between neighbouring devices the same number of tokens moves each way, at least one and at most 72, exactly 72 at some boundary in every draw. `dest_row`: the inverse of source_row. `slot_start`: equal for all slots of one document; every document holds at most 400 tokens, and one holds exactly 400.
All inputs are finite; a program needn't handle non-finite values.
Results may differ from the reference program's by a relative error of at most 0.0063.
Values may be sent and summed in bfloat16 or wider, within the bound.
No kernel may reach another device: no remote copies, remote signals or barrier semaphores. Data moves between devices by JAX's collectives and lax.ppermute only.
A program may use at most 64 MiB of HBM per device.

```python
import jax
import jax.numpy as jnp
from jax import lax

D = 4096
HD = 128
GROUP = 4
TOK_DEV = 512
KV_HEADS = 8
HEADS = 32
TOKENS = 32768


def moving_plan(key):
    cell_size = TOK_DEV // 8
    jitter = TOK_DEV // 64
    device_count = TOKENS // TOK_DEV
    longest = jax.random.randint(jax.random.fold_in(key, 11), (), 1, device_count - 1, dtype=jnp.int32)
    offset = jax.random.randint(jax.random.fold_in(key, 12), (), 0, device_count - 3, dtype=jnp.int32)
    busiest = (longest + 1 + offset) % (device_count - 1)
    shifts = jax.random.randint(jax.random.fold_in(key, 13), (device_count - 1,), -jitter, jitter + 1, dtype=jnp.int32)
    bounds = jnp.arange(device_count - 1, dtype=jnp.int32)
    shifts = jnp.where((bounds == longest - 1) | (bounds == longest), -jitter, shifts)
    shifts = jnp.where(bounds == busiest, jitter, shifts)
    moved = (cell_size + shifts).astype(jnp.int32)
    nothing = jnp.zeros((1,), jnp.int32)
    leading = jnp.concatenate([nothing, moved])
    trailing = jnp.concatenate([moved, nothing])
    devices = jnp.arange(device_count, dtype=jnp.int32)
    wiggle = jax.random.randint(jax.random.fold_in(key, 14), (device_count, 7), -jitter, jitter + 1, dtype=jnp.int32)
    coin_flip = jax.random.randint(jax.random.fold_in(key, 15), (device_count, 7), 0, 2, dtype=jnp.int32)
    line_index = jnp.arange(2, 7, dtype=jnp.int32)
    first_col = jnp.where(devices > 0, leading, cell_size + wiggle[:, 0])
    last_col = jnp.where(devices < device_count - 1, TOK_DEV - trailing, 7 * cell_size + wiggle[:, 6])
    inner_cut = line_index[None, :] * cell_size + wiggle[:, 1:6]
    keep_cut = (coin_flip[:, 1:6] == 1) & (devices[:, None] != longest)
    inner_cut = jnp.where(keep_cut, inner_cut, 0)
    cut_points = jnp.concatenate([jnp.zeros((device_count, 1), jnp.int32), first_col[:, None], inner_cut, last_col[:, None]], axis=1)
    position = jnp.arange(TOK_DEV, dtype=jnp.int32)
    below = cut_points[:, None, :] <= position[None, :, None]
    start_local = jnp.max(jnp.where(below, cut_points[:, None, :], 0), axis=2)
    doc_start = (start_local + devices[:, None] * TOK_DEV).reshape(TOKENS).astype(jnp.int32)
    slot_index = jnp.arange(TOKENS, dtype=jnp.int32)
    owner = slot_index // TOK_DEV
    local_pos = slot_index % TOK_DEV
    lead_here = leading[owner]
    trail_here = trailing[owner]
    source = jnp.where(local_pos < trail_here, slot_index + TOK_DEV, jnp.where(local_pos >= TOK_DEV - lead_here, slot_index - TOK_DEV, slot_index + lead_here - trail_here)).astype(jnp.int32)
    target = jnp.zeros((TOKENS,), jnp.int32).at[source].set(slot_index)
    first_token = doc_start[source].astype(jnp.int32)
    return (source, target, first_token)


def draw_source_row(key, part):
    return moving_plan(key)[0]


def draw_dest_row(key, part):
    return moving_plan(key)[1]


def draw_slot_start(key, part):
    return moving_plan(key)[2]


def draw_log_norm(key, part):
    source, target, first_token = moving_plan(key)
    key = jax.random.fold_in(key, 7)
    within = (source - first_token).astype(jnp.float32)
    center = jnp.log1p(within) + 0.5
    noise = jax.random.uniform(key, (HEADS, TOKENS), jnp.float32, -0.25, 0.25)
    return center[None, :] + noise


def steps_of(stream_key, extent, cuts, low, largest):
    def one(dim, blocks):
        steps = jax.random.uniform(jax.random.fold_in(jax.random.fold_in(stream_key, 6), dim), (blocks,), jnp.float32, low / len(cuts), largest / len(cuts))
        return jnp.repeat(jnp.exp(steps), extent[dim] // blocks).reshape((-1,) + (1,) * (len(extent) - dim - 1))

    level = one(*cuts[0])
    for cut in cuts[1:]:
        level = level * one(*cut)
    return level


def normal_values(own_key, shape, width, reach, pieces=(), held_as=jnp.bfloat16):
    entries = width * jax.random.normal(own_key, shape, jnp.float32)
    if pieces:
        entries = entries * steps_of(own_key, shape, pieces, -0.22, 0.18)
    return jnp.clip(entries, -reach, reach).astype(held_as)


def setup_inputs(seed: int = 0) -> dict:
    key_of = jax.random.split(jax.random.key(seed), 11)
    queries = normal_values(key_of[0], (TOKENS, HEADS * HD), 1.0, 6.0, ((0, 64), (1, 8)))
    keys = normal_values(key_of[1], (TOKENS, KV_HEADS * HD), 1.0, 6.0, ((0, 64), (1, 8)))
    values = normal_values(key_of[2], (TOKENS, KV_HEADS * HD), 1.0, 6.0, ((0, 64), (1, 8)))
    attn_out = normal_values(key_of[3], (TOKENS, HEADS * HD), 1.0, 6.0, ((0, 64), (1, 8)))
    grad_out = normal_values(key_of[4], (TOKENS, D), 4.0, 24.0, ((0, 64), (1, 8)))
    out_weight = normal_values(key_of[5], (D, HEADS * HD), D ** -0.5, 0.09375, ((0, 64), (1, 8)))
    log_norm = draw_log_norm(jax.random.fold_in(key_of[10], 71), 0)
    source_row = draw_source_row(jax.random.fold_in(key_of[10], 71), 0)
    dest_row = draw_dest_row(jax.random.fold_in(key_of[10], 71), 0)
    slot_start = draw_slot_start(jax.random.fold_in(key_of[10], 71), 0)
    return dict(queries=queries, keys=keys, values=values, attn_out=attn_out, grad_out=grad_out, out_weight=out_weight, log_norm=log_norm, source_row=source_row, dest_row=dest_row, slot_start=slot_start)


def backward_block(query_heads, head_grads, key_heads, value_heads, norm_heads, delta_heads, allowed):
    attn_scale = HD ** -0.5
    query_f = query_heads.astype(jnp.float32)
    grads_f = head_grads.astype(jnp.float32)
    keys_f = key_heads.astype(jnp.float32)
    values_f = value_heads.astype(jnp.float32)
    scores = jnp.einsum("pghe,jge->ghpj", query_f, keys_f) * attn_scale
    attn_prob = jnp.where(allowed[None, None], jnp.exp(scores - norm_heads[..., None]), jnp.float32(0.0))
    grad_prob = jnp.einsum("pghe,jge->ghpj", grads_f, values_f)
    grad_score = attn_prob * (grad_prob - delta_heads[..., None])
    prob_half = lax.optimization_barrier(attn_prob.astype(jnp.bfloat16)).astype(jnp.float32)
    score_half = lax.optimization_barrier(grad_score.astype(jnp.bfloat16)).astype(jnp.float32)
    value_grad = jnp.einsum("ghpj,pghe->jge", prob_half, grads_f)
    query_grad = jnp.einsum("ghpj,jge->pghe", score_half, keys_f)
    key_grad = jnp.einsum("ghpj,pghe->jge", score_half, query_f)
    return query_grad, key_grad, value_grad


def reference(queries, keys, values, attn_out, grad_out, out_weight, log_norm, source_row, dest_row, slot_start):
    attn_scale = HD ** -0.5
    grad_heads = jnp.dot(grad_out, out_weight, preferred_element_type=jnp.float32).astype(jnp.bfloat16)
    moved_queries = jnp.take(queries, source_row, axis=0)
    moved_keys = jnp.take(keys, source_row, axis=0)
    moved_values = jnp.take(values, source_row, axis=0)
    moved_grads = jnp.take(grad_heads, source_row, axis=0)
    product = moved_grads.astype(jnp.float32) * attn_out.astype(jnp.float32)
    row_delta = jnp.sum(product.reshape(TOKENS, HEADS, HD), axis=2).T
    block_count = TOKENS // TOK_DEV

    def one_block(inputs):
        query_rows, grad_rows, key_rows, value_rows, norm_rows, delta_rows, source_rows, start_rows = inputs
        allowed = (source_rows[None, :] >= start_rows[:, None]) & (source_rows[None, :] <= source_rows[:, None])
        query_grad, key_grad, value_grad = backward_block(
            query_rows.reshape(TOK_DEV, KV_HEADS, GROUP, HD),
            grad_rows.reshape(TOK_DEV, KV_HEADS, GROUP, HD),
            key_rows.reshape(TOK_DEV, KV_HEADS, HD),
            value_rows.reshape(TOK_DEV, KV_HEADS, HD),
            norm_rows.reshape(KV_HEADS, GROUP, TOK_DEV),
            delta_rows.reshape(KV_HEADS, GROUP, TOK_DEV),
            allowed)
        balanced_queries = (query_grad.reshape(TOK_DEV, HEADS * HD) * attn_scale).astype(jnp.bfloat16)
        balanced_keys = (key_grad.reshape(TOK_DEV, KV_HEADS * HD) * attn_scale).astype(jnp.bfloat16)
        balanced_values = value_grad.reshape(TOK_DEV, KV_HEADS * HD).astype(jnp.bfloat16)
        return balanced_queries, balanced_keys, balanced_values

    def blocks_of(matrix):
        return matrix.reshape(block_count, TOK_DEV, matrix.shape[1])

    def head_blocks(matrix):
        return matrix.reshape(HEADS, block_count, TOK_DEV).transpose(1, 0, 2)

    balanced = lax.map(one_block, (blocks_of(moved_queries), blocks_of(moved_grads), blocks_of(moved_keys), blocks_of(moved_values), head_blocks(log_norm), head_blocks(row_delta), source_row.reshape(block_count, TOK_DEV), slot_start.reshape(block_count, TOK_DEV)))
    grad_queries = jnp.take(balanced[0].reshape(TOKENS, HEADS * HD), dest_row, axis=0)
    grad_keys = jnp.take(balanced[1].reshape(TOKENS, KV_HEADS * HD), dest_row, axis=0)
    grad_values = jnp.take(balanced[2].reshape(TOKENS, KV_HEADS * HD), dest_row, axis=0)
    return grad_queries, grad_keys, grad_values
```

```python
import jax
import jax.numpy as jnp
from jax import lax
from jax.experimental import pallas as pl
from jax.experimental.pallas import tpu as pltpu
from jax.sharding import PartitionSpec as P

HD = 128
GROUP = 4
HALO = 80
BLK = 256
X, Z = 4, 8

NT = (((1,), (1,)), ((), ()))
TN = (((0,), (0,)), ((), ()))


def dot(a, b, dims=(((1,), (0,)), ((), ()))):
    return lax.dot_general(a, b, dims, preferred_element_type=jnp.float32)


def iota(shape, dim):
    return lax.broadcasted_iota(jnp.int32, shape, dim)


def send_kernel(first_ref, source_ref, start_ref, norm_ref, attn_ref, left_ref, right_ref, stats_ref, parts):
    first = first_ref[0]
    rows, width = attn_ref.shape
    source = source_ref[...]
    is_left = source < first
    is_right = source >= first + rows
    parts[...] = jnp.zeros_like(parts)
    rest = norm_ref[...]
    for part in range(3):
        half = rest.astype(jnp.bfloat16).astype(jnp.float32)
        parts[8 * part : 8 * part + GROUP, :] = half
        rest = rest - half
    start = start_ref[...]
    parts[24:25, :] = (start // 128).astype(jnp.float32)
    parts[32:33, :] = (start % 128).astype(jnp.float32)
    stats_ref[...] = parts[...].astype(jnp.bfloat16)
    until = (iota((rows, rows), 0) <= iota((rows, rows), 1)).astype(jnp.bfloat16)
    for mask, out_ref in ((is_left, left_ref), (is_right, right_ref)):
        flags = jnp.broadcast_to(jnp.where(mask, 1.0, 0.0), (16, rows))
        count = dot(flags.astype(jnp.bfloat16), until)[:1].astype(jnp.int32)
        place = jnp.where(mask, count - 1, -1)
        pick = jnp.where(iota((HALO, rows), 0) == place, 1.0, 0.0).astype(jnp.bfloat16)
        out_ref[:, :width] = dot(pick, attn_ref[...]).astype(jnp.bfloat16)
        out_ref[:, width:] = dot(pick, stats_ref[...], NT).astype(jnp.bfloat16)


def receive_kernel(first_ref, dest_ref, attn_ref, stats_ref, low_ref, high_ref, attn_out_ref, stats_out_ref):
    first = first_ref[0].astype(jnp.float32)
    rows, width = attn_ref.shape
    dest_row = dest_ref[...].astype(jnp.float32)
    dest_col = jnp.broadcast_to(dest_row, (128, rows)).T[:, :1]
    smaller = jnp.sum(jnp.where(dest_row < dest_col, 1.0, 0.0), axis=1, keepdims=True)
    below_high = jnp.sum(jnp.where(dest_row < first + rows, 1.0, 0.0), axis=1, keepdims=True)
    place_low = jnp.where(dest_col < first, smaller, -1.0).astype(jnp.int32)
    place_high = jnp.where(dest_col >= first + rows, smaller - below_high, -1.0).astype(jnp.int32)
    place_here = (dest_col - first).astype(jnp.int32)
    here = jnp.where(iota((rows, rows), 1) == place_here, 1.0, 0.0).astype(jnp.bfloat16)
    low = jnp.where(iota((rows, HALO), 1) == place_low, 1.0, 0.0).astype(jnp.bfloat16)
    high = jnp.where(iota((rows, HALO), 1) == place_high, 1.0, 0.0).astype(jnp.bfloat16)
    moved = dot(here, attn_ref[...]) + dot(low, low_ref[:, :width]) + dot(high, high_ref[:, :width])
    attn_out_ref[...] = moved.astype(jnp.bfloat16)
    stats_t = (
        dot(stats_ref[...], here, NT)
        + dot(low_ref[:, width:].T, low, NT)
        + dot(high_ref[:, width:].T, high, NT)
    )
    stats_out_ref[0:8, :] = stats_t[0:8] + stats_t[8:16] + stats_t[16:24]
    stats_out_ref[8:16, :] = stats_t[24:32] * 128.0 + stats_t[32:40] - first


def tiles_of(rows):
    return [(i, j) for i in range(rows // BLK) for j in range(i + 1)]


def attend_kernel(
    me_ref, grad_ref, near_ref, far_ref, near_other_ref, far_other_ref,
    query_in, key_in, value_in, attn_in, stats_in,
    dq_ref, dk_ref, dv_ref,
    grad_buf, weight_buf, query_ref, key_ref, value_ref, attn_ref, stats_ref,
    total, prob, heads, grad_sems, weight_sems, sems,
):
    parts, rows, depth = grad_ref.shape
    scale = HD**-0.5
    my_x, my_z, my_core = me_ref[0], me_ref[1], me_ref[2]
    ins = [
        pltpu.make_async_copy(source, target, sems.at[index])
        for index, (source, target) in enumerate(
            ((query_in, query_ref), (key_in, key_ref), (stats_in, stats_ref), (value_in, value_ref), (attn_in, attn_ref))
        )
    ]
    for copy in ins:
        copy.start()
    for refs, core in (((near_ref, far_ref), my_core), ((near_other_ref, far_other_ref), 1 - my_core)):
        for piece_ref, z_steps in zip(refs, (NEAR, FAR)):
            for index, step in enumerate(z_steps):
                z = lax.rem(my_z + step + Z, Z)
                pltpu.make_async_copy(
                    piece_ref.at[index], weight_buf.at[z, :, core], weight_sems.at[2 * z + core]
                ).start()
    grads = []
    for half in range(2):
        for index, step in enumerate(COLUMN):
            part = 2 * (my_x ^ step) + half
            copy = pltpu.make_async_copy(grad_ref.at[part], grad_buf.at[index, half], grad_sems.at[index, half])
            copy.start()
            grads.append(copy)
    for copy in ins[:3]:
        copy.wait()
    for i, j in tiles_of(rows):
        tokens, others = pl.ds(i * BLK, BLK), pl.ds(j * BLK, BLK)
        begin = stats_ref[8:9, tokens].astype(jnp.int32)
        other = iota((BLK, BLK), 0) + j * BLK
        token = iota((BLK, BLK), 1) + i * BLK
        allowed = (begin <= other) & (other <= token)
        for h in range(GROUP):
            score = dot(key_ref[others, :], query_ref[tokens, h * HD : (h + 1) * HD], NT) * scale
            prob[h, others, tokens] = jnp.where(allowed, jnp.exp(score - stats_ref[h : h + 1, tokens]), 0.0)
    for z in range(Z):
        half, place = z // (Z // 2), z % (Z // 2)
        for core in range(2):
            pltpu.make_async_copy(near_ref.at[0], weight_buf.at[z, :, core], weight_sems.at[2 * z + core]).wait()
        if place == 0:
            for copy in grads[half * X : (half + 1) * X]:
                copy.wait()
        left = jnp.concatenate([grad_buf[x, half, :, place * 128 : (place + 1) * 128] for x in range(X)], axis=1)
        product = dot(left, weight_buf[z].reshape(depth, -1))
        if z == 0:
            total[...] = product
        else:
            total[...] += product
    for copy in ins[3:]:
        copy.wait()
    heads[...] = total[...].astype(jnp.bfloat16)
    delta = jnp.zeros((rows, HD), jnp.float32)
    for h in range(GROUP):
        cols = slice(h * HD, (h + 1) * HD)
        product = heads[:, cols].astype(jnp.float32) * attn_ref[:, cols].astype(jnp.float32)
        delta = jnp.where(iota((rows, HD), 1) == h, jnp.sum(product, axis=1, keepdims=True), delta)
    delta = delta.T
    key_total = [0.0] * (rows // BLK)
    value_total = [0.0] * (rows // BLK)
    query_total = {}
    for i, j in tiles_of(rows):
        tokens, others = pl.ds(i * BLK, BLK), pl.ds(j * BLK, BLK)
        for h in range(GROUP):
            cols = slice(h * HD, (h + 1) * HD)
            grads = heads[tokens, cols]
            p = prob[h, others, tokens]
            grad_prob = dot(value_ref[others, :], grads, NT)
            grad_score = p * (grad_prob - delta[h : h + 1, i * BLK : (i + 1) * BLK])
            score_half = grad_score.astype(jnp.bfloat16)
            value_total[j] += dot(p.astype(jnp.bfloat16), grads)
            key_total[j] += dot(score_half, query_ref[tokens, cols])
            update = dot(score_half, key_ref[others, :], TN)
            query_total[i, h] = query_total[i, h] + update if (i, h) in query_total else update
    for (i, h), value in query_total.items():
        dq_ref[pl.ds(i * BLK, BLK), h * HD : (h + 1) * HD] = (value * scale).astype(jnp.bfloat16)
    for j in range(rows // BLK):
        dk_ref[pl.ds(j * BLK, BLK), :] = (key_total[j] * scale).astype(jnp.bfloat16)
        dv_ref[pl.ds(j * BLK, BLK), :] = value_total[j].astype(jnp.bfloat16)


def move(block, target):
    pairs = []
    for x in range(X):
        for z in range(Z):
            for core in range(2):
                tx, tz, tc = target(x, z, core)
                pairs.append(((x * Z + z) * 2 + core, ((tx % X) * Z + tz % Z) * 2 + tc))
    return lax.ppermute(block, "dp", pairs)


SMEM = pl.BlockSpec(memory_space=pltpu.SMEM)
VMEM = pl.BlockSpec(memory_space=pltpu.VMEM)
HBM = pl.BlockSpec(memory_space=pltpu.HBM)


def after(value, *others):
    return lax.optimization_barrier((value, *others))[0]


COLUMN = (0, 1, 3, 2)
NEAR, FAR = (0, -1, 1, -2, 2), (-3, 3, 4)


def on_device(
    queries, keys, values, attn_out, grad_out, out_weight, log_norm, source_row, dest_row, slot_start
):
    rows, width = queries.shape
    key_width = keys.shape[1]
    all_grad = lax.all_gather(grad_out, "tensor", axis=0, tiled=False)

    me = lax.axis_index("dp").astype(jnp.int32)
    first = (me * rows).reshape(1)
    place = jnp.stack([me // (2 * Z), (me // 2) % Z, me % 2])
    message = jax.ShapeDtypeStruct((HALO, width + 128), jnp.bfloat16)
    to_low, to_high, stats = pl.pallas_call(
        send_kernel,
        out_shape=(message, message, jax.ShapeDtypeStruct((128, rows), jnp.bfloat16)),
        in_specs=[SMEM] + [VMEM] * 4,
        out_specs=(VMEM,) * 3,
        scratch_shapes=[pltpu.VMEM((128, rows), jnp.float32)],
        cost_estimate=pl.CostEstimate(flops=2 * 2 * HALO * rows * 640, bytes_accessed=1 << 20, transcendentals=0),
        name="send_rows",
    )(first, source_row[None], slot_start[None], log_norm, attn_out)

    up = lambda x, z, c: (x, z + 1, c)
    down = lambda x, z, c: (x, z - 1, c)
    other = lambda x, z, c: (x, z, 1 - c)
    pair = jnp.concatenate([out_weight, move(out_weight, lambda x, z, c: (x ^ 1, z, c))], axis=0)
    pair = after(pair, to_low, to_high)
    forward = [(i, i + 1) for i in range(lax.axis_size("dp") - 1)]
    from_low = lax.ppermute(to_high, "dp", forward)
    from_high = lax.ppermute(to_low, "dp", [(b, a) for a, b in forward])
    column = jnp.concatenate([pair, move(pair, lambda x, z, c: (3 - x, z, c))], axis=0)
    up1 = move(column, up)
    attn_packed, stats_packed = pl.pallas_call(
        receive_kernel,
        out_shape=(
            jax.ShapeDtypeStruct((rows, width), jnp.bfloat16),
            jax.ShapeDtypeStruct((16, rows), jnp.float32),
        ),
        in_specs=[SMEM] + [VMEM] * 5,
        out_specs=(VMEM, VMEM),
        cost_estimate=pl.CostEstimate(flops=2 * rows * rows * 640, bytes_accessed=2 << 20, transcendentals=0),
        name="receive_rows",
    )(first, dest_row[None], attn_out, stats, from_low, from_high)
    down1 = move(column, down)
    up2, down2 = move(up1, up), move(after(down1, attn_packed, stats_packed), down)
    up3, down3 = move(up2, up), move(down2, down)
    up4 = move(up3, up)
    near = jnp.concatenate([column, up1, down1, up2, down2], axis=0)
    near_other = move(near, other)
    far = jnp.concatenate([up3, down3, up4], axis=0)
    far_other = move(far, other)
    pieces = [piece.reshape(-1, X, *out_weight.shape) for piece in (near, far, near_other, far_other)]

    parts, _, depth = all_grad.shape
    return pl.pallas_call(
        attend_kernel,
        out_shape=(
            jax.ShapeDtypeStruct((rows, width), jnp.bfloat16),
            jax.ShapeDtypeStruct((rows, key_width), jnp.bfloat16),
            jax.ShapeDtypeStruct((rows, key_width), jnp.bfloat16),
        ),
        in_specs=[SMEM] + [HBM] * 10,
        out_specs=(VMEM, VMEM, VMEM),
        scratch_shapes=[
            pltpu.VMEM((X, 2, rows, depth), jnp.bfloat16),
            pltpu.VMEM((Z, X, 2, *out_weight.shape), jnp.bfloat16),
            pltpu.VMEM(queries.shape, jnp.bfloat16),
            pltpu.VMEM(keys.shape, jnp.bfloat16),
            pltpu.VMEM(values.shape, jnp.bfloat16),
            pltpu.VMEM(attn_out.shape, jnp.bfloat16),
            pltpu.VMEM(stats_packed.shape, jnp.float32),
            pltpu.VMEM((rows, width), jnp.float32),
            pltpu.VMEM((GROUP, rows, rows), jnp.float32),
            pltpu.VMEM((rows, width), jnp.bfloat16),
            pltpu.SemaphoreType.DMA((X, 2)),
            pltpu.SemaphoreType.DMA((2 * Z,)),
            pltpu.SemaphoreType.DMA((5,)),
        ],
        compiler_params=pltpu.CompilerParams(vmem_limit_bytes=60 << 20),
        cost_estimate=pl.CostEstimate(flops=4 << 30, bytes_accessed=12 << 20, transcendentals=1 << 20),
        name="attend",
    )(place, all_grad, *pieces, queries, keys, values, attn_packed, stats_packed)


def solution(mesh):
    in_specs = (P("dp", "tensor"),) * 6 + (P("tensor", "dp"), P("dp"), P("dp"), P("dp"))
    out_specs = (P("dp", "tensor"),) * 3
    return jax.shard_map(
        on_device, mesh=mesh, in_specs=in_specs, out_specs=out_specs, check_vma=False
    )
```

```python
import jax
import jax.numpy as jnp
from jax import lax
from jax.experimental import pallas as pl
from jax.experimental.pallas import tpu as pltpu
from jax.sharding import PartitionSpec as P

HD = 128
GROUP = 4
HALO = 80
BLK = 256
X, Z = 4, 8

NT = (((1,), (1,)), ((), ()))
TN = (((0,), (0,)), ((), ()))


def dot(a, b, dims=(((1,), (0,)), ((), ()))):
    return lax.dot_general(a, b, dims, preferred_element_type=jnp.float32)


def iota(shape, dim):
    return lax.broadcasted_iota(jnp.int32, shape, dim)


def send_kernel(first_ref, source_ref, start_ref, norm_ref, attn_ref, left_ref, right_ref, stats_ref, parts):
    first = first_ref[0]
    rows, width = attn_ref.shape
    source = source_ref[...]
    is_left = source < first
    is_right = source >= first + rows
    parts[...] = jnp.zeros_like(parts)
    rest = norm_ref[...]
    for part in range(3):
        half = rest.astype(jnp.bfloat16).astype(jnp.float32)
        parts[8 * part : 8 * part + GROUP, :] = half
        rest = rest - half
    start = start_ref[...]
    parts[24:25, :] = (start // 128).astype(jnp.float32)
    parts[32:33, :] = (start % 128).astype(jnp.float32)
    stats_ref[...] = parts[...].astype(jnp.bfloat16)
    until = (iota((rows, rows), 0) <= iota((rows, rows), 1)).astype(jnp.bfloat16)
    for mask, out_ref in ((is_left, left_ref), (is_right, right_ref)):
        flags = jnp.broadcast_to(jnp.where(mask, 1.0, 0.0), (16, rows))
        count = dot(flags.astype(jnp.bfloat16), until)[:1].astype(jnp.int32)
        place = jnp.where(mask, count - 1, -1)
        pick = jnp.where(iota((HALO, rows), 0) == place, 1.0, 0.0).astype(jnp.bfloat16)
        out_ref[:, :width] = dot(pick, attn_ref[...]).astype(jnp.bfloat16)
        out_ref[:, width:] = dot(pick, stats_ref[...], NT).astype(jnp.bfloat16)


def receive_kernel(first_ref, dest_ref, attn_ref, stats_ref, low_ref, high_ref, attn_out_ref, stats_out_ref):
    first = first_ref[0].astype(jnp.float32)
    rows, width = attn_ref.shape
    dest_row = dest_ref[...].astype(jnp.float32)
    dest_col = jnp.broadcast_to(dest_row, (128, rows)).T[:, :1]
    smaller = jnp.sum(jnp.where(dest_row < dest_col, 1.0, 0.0), axis=1, keepdims=True)
    below_high = jnp.sum(jnp.where(dest_row < first + rows, 1.0, 0.0), axis=1, keepdims=True)
    place_low = jnp.where(dest_col < first, smaller, -1.0).astype(jnp.int32)
    place_high = jnp.where(dest_col >= first + rows, smaller - below_high, -1.0).astype(jnp.int32)
    place_here = (dest_col - first).astype(jnp.int32)
    here = jnp.where(iota((rows, rows), 1) == place_here, 1.0, 0.0).astype(jnp.bfloat16)
    low = jnp.where(iota((rows, HALO), 1) == place_low, 1.0, 0.0).astype(jnp.bfloat16)
    high = jnp.where(iota((rows, HALO), 1) == place_high, 1.0, 0.0).astype(jnp.bfloat16)
    moved = dot(here, attn_ref[...]) + dot(low, low_ref[:, :width]) + dot(high, high_ref[:, :width])
    attn_out_ref[...] = moved.astype(jnp.bfloat16)
    stats_t = (
        dot(stats_ref[...], here, NT)
        + dot(low_ref[:, width:].T, low, NT)
        + dot(high_ref[:, width:].T, high, NT)
    )
    stats_out_ref[0:8, :] = stats_t[0:8] + stats_t[8:16] + stats_t[16:24]
    stats_out_ref[8:16, :] = stats_t[24:32] * 128.0 + stats_t[32:40] - first


def tiles_of(rows):
    return [(i, j) for i in range(rows // BLK) for j in range(i + 1)]


def attend_kernel(
    me_ref, grad_ref, near_ref, far_ref, near_other_ref, far_other_ref,
    query_in, key_in, value_in, attn_in, stats_in,
    dq_ref, dk_ref, dv_ref,
    grad_buf, weight_buf, query_ref, key_ref, value_ref, attn_ref, stats_ref,
    total, prob, heads, grad_sems, weight_sems, sems,
):
    parts, rows, depth = grad_ref.shape
    scale = HD**-0.5
    my_x, my_z, my_core = me_ref[0], me_ref[1], me_ref[2]
    ins = [
        pltpu.make_async_copy(source, target, sems.at[index])
        for index, (source, target) in enumerate(
            ((query_in, query_ref), (key_in, key_ref), (stats_in, stats_ref), (value_in, value_ref), (attn_in, attn_ref))
        )
    ]
    for copy in ins:
        copy.start()
    batches = []
    for batch in range(2):
        own = slice(batch * X // 2, (batch + 1) * X // 2)
        copies = []
        for refs, core in (((near_ref, far_ref), my_core), ((near_other_ref, far_other_ref), 1 - my_core)):
            for piece_ref, z_steps in zip(refs, (NEAR, FAR)):
                for index, step in enumerate(z_steps):
                    z = lax.rem(my_z + step + Z, Z)
                    copies.append(
                        pltpu.make_async_copy(
                            piece_ref.at[index, own], weight_buf.at[z, own, core], weight_sems.at[batch, len(copies)]
                        )
                    )
        for index in range(own.start, own.stop):
            for half in range(2):
                part = 2 * (my_x ^ COLUMN[index]) + half
                copies.append(
                    pltpu.make_async_copy(grad_ref.at[part], grad_buf.at[index, half], grad_sems.at[index, half])
                )
        batches.append(copies)
    for copy in batches[0]:
        copy.start()
    for copy in ins[:3]:
        copy.wait()
    for i, j in tiles_of(rows):
        tokens, others = pl.ds(i * BLK, BLK), pl.ds(j * BLK, BLK)
        begin = stats_ref[8:9, tokens].astype(jnp.int32)
        other = iota((BLK, BLK), 0) + j * BLK
        token = iota((BLK, BLK), 1) + i * BLK
        allowed = (begin <= other) & (other <= token)
        for h in range(GROUP):
            score = dot(key_ref[others, :], query_ref[tokens, h * HD : (h + 1) * HD], NT) * scale
            prob[h, others, tokens] = jnp.where(allowed, jnp.exp(score - stats_ref[h : h + 1, tokens]), 0.0)
    for copy in batches[1]:
        copy.start()
    for batch, copies in enumerate(batches):
        for copy in copies:
            copy.wait()
        product = 0.0
        for index in range(batch * X // 2, (batch + 1) * X // 2):
            for half in range(2):
                right = weight_buf[half * (Z // 2) : (half + 1) * (Z // 2), index].reshape(depth, -1)
                product += dot(grad_buf[index, half], right)
        if batch == 0:
            total[...] = product
        else:
            heads[...] = (total[...] + product).astype(jnp.bfloat16)
    for copy in ins[3:]:
        copy.wait()
    delta = jnp.zeros((rows, HD), jnp.float32)
    for h in range(GROUP):
        cols = slice(h * HD, (h + 1) * HD)
        product = heads[:, cols].astype(jnp.float32) * attn_ref[:, cols].astype(jnp.float32)
        delta = jnp.where(iota((rows, HD), 1) == h, jnp.sum(product, axis=1, keepdims=True), delta)
    delta = delta.T
    key_total = [0.0] * (rows // BLK)
    value_total = [0.0] * (rows // BLK)
    query_total = {}
    for i, j in tiles_of(rows):
        tokens, others = pl.ds(i * BLK, BLK), pl.ds(j * BLK, BLK)
        for h in range(GROUP):
            cols = slice(h * HD, (h + 1) * HD)
            grads = heads[tokens, cols]
            p = prob[h, others, tokens]
            grad_prob = dot(value_ref[others, :], grads, NT)
            grad_score = p * (grad_prob - delta[h : h + 1, i * BLK : (i + 1) * BLK])
            score_half = grad_score.astype(jnp.bfloat16)
            value_total[j] += dot(p.astype(jnp.bfloat16), grads)
            key_total[j] += dot(score_half, query_ref[tokens, cols])
            update = dot(score_half, key_ref[others, :], TN)
            query_total[i, h] = query_total[i, h] + update if (i, h) in query_total else update
    for (i, h), value in query_total.items():
        dq_ref[pl.ds(i * BLK, BLK), h * HD : (h + 1) * HD] = (value * scale).astype(jnp.bfloat16)
    for j in range(rows // BLK):
        dk_ref[pl.ds(j * BLK, BLK), :] = (key_total[j] * scale).astype(jnp.bfloat16)
        dv_ref[pl.ds(j * BLK, BLK), :] = value_total[j].astype(jnp.bfloat16)


def move(block, target):
    pairs = []
    for x in range(X):
        for z in range(Z):
            for core in range(2):
                tx, tz, tc = target(x, z, core)
                pairs.append(((x * Z + z) * 2 + core, ((tx % X) * Z + tz % Z) * 2 + tc))
    return lax.ppermute(block, "dp", pairs)


SMEM = pl.BlockSpec(memory_space=pltpu.SMEM)
VMEM = pl.BlockSpec(memory_space=pltpu.VMEM)
HBM = pl.BlockSpec(memory_space=pltpu.HBM)


def after(value, *others):
    return lax.optimization_barrier((value, *others))[0]


COLUMN = (0, 1, 3, 2)
NEAR, FAR = (0, -1, 1, -2, 2), (-3, 3, 4)


def attend(place, all_grad, near, far, near_other, far_other, queries, keys, values, attn, stats):
    parts, rows, depth = all_grad.shape
    width, key_width = queries.shape[1], keys.shape[1]
    return pl.pallas_call(
        attend_kernel,
        out_shape=(
            jax.ShapeDtypeStruct((rows, width), jnp.bfloat16),
            jax.ShapeDtypeStruct((rows, key_width), jnp.bfloat16),
            jax.ShapeDtypeStruct((rows, key_width), jnp.bfloat16),
        ),
        in_specs=[SMEM] + [HBM] * 10,
        out_specs=(VMEM, VMEM, VMEM),
        scratch_shapes=[
            pltpu.VMEM((X, 2, rows, depth), jnp.bfloat16),
            pltpu.VMEM((Z, X, 2, *near.shape[2:]), jnp.bfloat16),
            pltpu.VMEM(queries.shape, jnp.bfloat16),
            pltpu.VMEM(keys.shape, jnp.bfloat16),
            pltpu.VMEM(values.shape, jnp.bfloat16),
            pltpu.VMEM(attn.shape, jnp.bfloat16),
            pltpu.VMEM(stats.shape, jnp.float32),
            pltpu.VMEM((rows, width), jnp.float32),
            pltpu.VMEM((GROUP, rows, rows), jnp.float32),
            pltpu.VMEM((rows, width), jnp.bfloat16),
            pltpu.SemaphoreType.DMA((X, 2)),
            pltpu.SemaphoreType.DMA((2, 2 * Z)),
            pltpu.SemaphoreType.DMA((5,)),
        ],
        compiler_params=pltpu.CompilerParams(vmem_limit_bytes=60 << 20),
        cost_estimate=pl.CostEstimate(flops=4 << 30, bytes_accessed=12 << 20, transcendentals=1 << 20),
        name="attend",
    )(place, all_grad, near, far, near_other, far_other, queries, keys, values, attn, stats)


def on_device(
    queries, keys, values, attn_out, grad_out, out_weight, log_norm, source_row, dest_row, slot_start
):
    rows, width = queries.shape
    key_width = keys.shape[1]
    all_grad = lax.all_gather(grad_out, "tensor", axis=0, tiled=False)

    me = lax.axis_index("dp").astype(jnp.int32)
    first = (me * rows).reshape(1)
    place = jnp.stack([me // (2 * Z), (me // 2) % Z, me % 2])
    message = jax.ShapeDtypeStruct((HALO, width + 128), jnp.bfloat16)
    to_low, to_high, stats = pl.pallas_call(
        send_kernel,
        out_shape=(message, message, jax.ShapeDtypeStruct((128, rows), jnp.bfloat16)),
        in_specs=[SMEM] + [VMEM] * 4,
        out_specs=(VMEM,) * 3,
        scratch_shapes=[pltpu.VMEM((128, rows), jnp.float32)],
        cost_estimate=pl.CostEstimate(flops=2 * 2 * HALO * rows * 640, bytes_accessed=1 << 20, transcendentals=0),
        name="send_rows",
    )(first, source_row[None], slot_start[None], log_norm, attn_out)

    up = lambda x, z, c: (x, z + 1, c)
    down = lambda x, z, c: (x, z - 1, c)
    other = lambda x, z, c: (x, z, 1 - c)
    pair = jnp.concatenate([out_weight, move(out_weight, lambda x, z, c: (x ^ 1, z, c))], axis=0)
    column = jnp.concatenate([pair, move(pair, lambda x, z, c: (3 - x, z, c))], axis=0)
    column = after(column, to_low, to_high)
    up1, down1 = move(column, up), move(column, down)
    up2, down2 = move(up1, up), move(down1, down)
    up3 = move(up2, up)
    near = jnp.concatenate([column, up1, down1, up2, down2], axis=0)
    near_other = move(near, other)
    down3 = move(down2, down)
    up4 = move(up3, up)
    to_low, to_high = lax.optimization_barrier((to_low, to_high, down3))[:2]
    forward = [(i, i + 1) for i in range(lax.axis_size("dp") - 1)]
    from_low = lax.ppermute(to_high, "dp", forward)
    from_high = lax.ppermute(to_low, "dp", [(b, a) for a, b in forward])
    attn_packed, stats_packed = pl.pallas_call(
        receive_kernel,
        out_shape=(
            jax.ShapeDtypeStruct((rows, width), jnp.bfloat16),
            jax.ShapeDtypeStruct((16, rows), jnp.float32),
        ),
        in_specs=[SMEM] + [VMEM] * 5,
        out_specs=(VMEM, VMEM),
        cost_estimate=pl.CostEstimate(flops=2 * rows * rows * 640, bytes_accessed=2 << 20, transcendentals=0),
        name="receive_rows",
    )(first, dest_row[None], attn_out, stats, from_low, from_high)
    far = jnp.concatenate([up3, after(down3, attn_packed, stats_packed), up4], axis=0)
    far_other = move(far, other)
    pieces = [piece.reshape(-1, X, *out_weight.shape) for piece in (near, far, near_other, far_other)]

    return attend(place, all_grad, *pieces, queries, keys, values, attn_packed, stats_packed)


def solution(mesh):
    in_specs = (P("dp", "tensor"),) * 6 + (P("tensor", "dp"), P("dp"), P("dp"), P("dp"))
    out_specs = (P("dp", "tensor"),) * 3
    return jax.shard_map(
        on_device, mesh=mesh, in_specs=in_specs, out_specs=out_specs, check_vma=False
    )
```

```python
import jax
import jax.numpy as jnp
from jax import lax
from jax.experimental import pallas as pl
from jax.experimental.pallas import tpu as pltpu
from jax.sharding import PartitionSpec as P

HD = 128
GROUP = 4
HALO = 80
BLK = 256
X, Z = 4, 8

NT = (((1,), (1,)), ((), ()))
TN = (((0,), (0,)), ((), ()))


def dot(a, b, dims=(((1,), (0,)), ((), ()))):
    return lax.dot_general(a, b, dims, preferred_element_type=jnp.float32)


def iota(shape, dim):
    return lax.broadcasted_iota(jnp.int32, shape, dim)


def send_kernel(first_ref, source_ref, start_ref, norm_ref, attn_ref, left_ref, right_ref, stats_ref, parts):
    first = first_ref[0]
    rows, width = attn_ref.shape
    source = source_ref[...]
    is_left = source < first
    is_right = source >= first + rows
    parts[...] = jnp.zeros_like(parts)
    rest = norm_ref[...]
    for part in range(3):
        half = rest.astype(jnp.bfloat16).astype(jnp.float32)
        parts[8 * part : 8 * part + GROUP, :] = half
        rest = rest - half
    start = start_ref[...]
    parts[24:25, :] = (start // 128).astype(jnp.float32)
    parts[32:33, :] = (start % 128).astype(jnp.float32)
    stats_ref[...] = parts[...].astype(jnp.bfloat16)
    until = (iota((rows, rows), 0) <= iota((rows, rows), 1)).astype(jnp.bfloat16)
    for mask, out_ref in ((is_left, left_ref), (is_right, right_ref)):
        flags = jnp.broadcast_to(jnp.where(mask, 1.0, 0.0), (16, rows))
        count = dot(flags.astype(jnp.bfloat16), until)[:1].astype(jnp.int32)
        place = jnp.where(mask, count - 1, -1)
        pick = jnp.where(iota((HALO, rows), 0) == place, 1.0, 0.0).astype(jnp.bfloat16)
        out_ref[:, :width] = dot(pick, attn_ref[...]).astype(jnp.bfloat16)
        out_ref[:, width:] = dot(pick, stats_ref[...], NT).astype(jnp.bfloat16)


def receive_kernel(first_ref, dest_ref, attn_ref, stats_ref, low_ref, high_ref, attn_out_ref, stats_out_ref):
    first = first_ref[0].astype(jnp.float32)
    rows, width = attn_ref.shape
    dest_row = dest_ref[...].astype(jnp.float32)
    dest_col = jnp.broadcast_to(dest_row, (128, rows)).T[:, :1]
    smaller = jnp.sum(jnp.where(dest_row < dest_col, 1.0, 0.0), axis=1, keepdims=True)
    below_high = jnp.sum(jnp.where(dest_row < first + rows, 1.0, 0.0), axis=1, keepdims=True)
    place_low = jnp.where(dest_col < first, smaller, -1.0).astype(jnp.int32)
    place_high = jnp.where(dest_col >= first + rows, smaller - below_high, -1.0).astype(jnp.int32)
    place_here = (dest_col - first).astype(jnp.int32)
    here = jnp.where(iota((rows, rows), 1) == place_here, 1.0, 0.0).astype(jnp.bfloat16)
    low = jnp.where(iota((rows, HALO), 1) == place_low, 1.0, 0.0).astype(jnp.bfloat16)
    high = jnp.where(iota((rows, HALO), 1) == place_high, 1.0, 0.0).astype(jnp.bfloat16)
    moved = dot(here, attn_ref[...]) + dot(low, low_ref[:, :width]) + dot(high, high_ref[:, :width])
    attn_out_ref[...] = moved.astype(jnp.bfloat16)
    stats_t = (
        dot(stats_ref[...], here, NT)
        + dot(low_ref[:, width:].T, low, NT)
        + dot(high_ref[:, width:].T, high, NT)
    )
    stats_out_ref[0:8, :] = stats_t[0:8] + stats_t[8:16] + stats_t[16:24]
    stats_out_ref[8:16, :] = stats_t[24:32] * 128.0 + stats_t[32:40] - first


def tiles_of(rows):
    return [(i, j) for i in range(rows // BLK) for j in range(i + 1)]


def attend_kernel(
    me_ref, grad_ref, near_ref, far_ref, near_other_ref, far_other_ref,
    query_in, key_in, value_in, attn_in, stats_in,
    dq_ref, dk_ref, dv_ref,
    grad_buf, weight_buf, query_ref, key_ref, value_ref, attn_ref, stats_ref,
    total, prob, heads, grad_sems, weight_sems, sems,
):
    parts, rows, depth = grad_ref.shape
    scale = HD**-0.5
    my_x, my_z, my_core = me_ref[0], me_ref[1], me_ref[2]
    ins = [
        pltpu.make_async_copy(source, target, sems.at[index])
        for index, (source, target) in enumerate(
            ((query_in, query_ref), (key_in, key_ref), (stats_in, stats_ref), (value_in, value_ref), (attn_in, attn_ref))
        )
    ]
    for copy in ins:
        copy.start()
    batches = []
    for batch in range(2):
        own = slice(batch * X // 2, (batch + 1) * X // 2)
        copies = []
        for refs, core in (((near_ref, far_ref), my_core), ((near_other_ref, far_other_ref), 1 - my_core)):
            for piece_ref, z_steps in zip(refs, (NEAR, FAR)):
                for index, step in enumerate(z_steps):
                    z = lax.rem(my_z + step + Z, Z)
                    copies.append(
                        pltpu.make_async_copy(
                            piece_ref.at[index, own], weight_buf.at[z, own, core], weight_sems.at[batch, len(copies)]
                        )
                    )
        for index in range(own.start, own.stop):
            for half in range(2):
                part = 2 * (my_x ^ COLUMN[index]) + half
                copies.append(
                    pltpu.make_async_copy(grad_ref.at[part], grad_buf.at[index, half], grad_sems.at[index, half])
                )
        batches.append(copies)
    for copy in batches[0]:
        copy.start()
    for copy in ins[:3]:
        copy.wait()
    for i, j in tiles_of(rows):
        tokens, others = pl.ds(i * BLK, BLK), pl.ds(j * BLK, BLK)
        begin = stats_ref[8:9, tokens].astype(jnp.int32)
        other = iota((BLK, BLK), 0) + j * BLK
        token = iota((BLK, BLK), 1) + i * BLK
        allowed = (begin <= other) & (other <= token)
        for h in range(GROUP):
            score = dot(key_ref[others, :], query_ref[tokens, h * HD : (h + 1) * HD], NT) * scale
            prob[h, others, tokens] = jnp.where(allowed, jnp.exp(score - stats_ref[h : h + 1, tokens]), 0.0)
    for copy in batches[1]:
        copy.start()
    for batch, copies in enumerate(batches):
        for copy in copies:
            copy.wait()
        product = 0.0
        for index in range(batch * X // 2, (batch + 1) * X // 2):
            for half in range(2):
                right = weight_buf[half * (Z // 2) : (half + 1) * (Z // 2), index].reshape(depth, -1)
                product += dot(grad_buf[index, half], right)
        if batch == 0:
            total[...] = product
        else:
            heads[...] = (total[...] + product).astype(jnp.bfloat16)
    for copy in ins[3:]:
        copy.wait()
    delta = jnp.zeros((rows, HD), jnp.float32)
    for h in range(GROUP):
        cols = slice(h * HD, (h + 1) * HD)
        product = heads[:, cols].astype(jnp.float32) * attn_ref[:, cols].astype(jnp.float32)
        delta = jnp.where(iota((rows, HD), 1) == h, jnp.sum(product, axis=1, keepdims=True), delta)
    delta = delta.T
    key_total = [0.0] * (rows // BLK)
    value_total = [0.0] * (rows // BLK)
    query_total = {}
    for i, j in tiles_of(rows):
        tokens, others = pl.ds(i * BLK, BLK), pl.ds(j * BLK, BLK)
        for h in range(GROUP):
            cols = slice(h * HD, (h + 1) * HD)
            grads = heads[tokens, cols]
            p = prob[h, others, tokens]
            grad_prob = dot(value_ref[others, :], grads, NT)
            grad_score = p * (grad_prob - delta[h : h + 1, i * BLK : (i + 1) * BLK])
            score_half = grad_score.astype(jnp.bfloat16)
            value_total[j] += dot(p.astype(jnp.bfloat16), grads)
            key_total[j] += dot(score_half, query_ref[tokens, cols])
            update = dot(score_half, key_ref[others, :], TN)
            query_total[i, h] = query_total[i, h] + update if (i, h) in query_total else update
    for (i, h), value in query_total.items():
        dq_ref[pl.ds(i * BLK, BLK), h * HD : (h + 1) * HD] = (value * scale).astype(jnp.bfloat16)
    for j in range(rows // BLK):
        dk_ref[pl.ds(j * BLK, BLK), :] = (key_total[j] * scale).astype(jnp.bfloat16)
        dv_ref[pl.ds(j * BLK, BLK), :] = value_total[j].astype(jnp.bfloat16)


def move(block, target):
    pairs = []
    for x in range(X):
        for z in range(Z):
            for core in range(2):
                tx, tz, tc = target(x, z, core)
                pairs.append(((x * Z + z) * 2 + core, ((tx % X) * Z + tz % Z) * 2 + tc))
    return lax.ppermute(block, "dp", pairs)


SMEM = pl.BlockSpec(memory_space=pltpu.SMEM)
VMEM = pl.BlockSpec(memory_space=pltpu.VMEM)
HBM = pl.BlockSpec(memory_space=pltpu.HBM)


def after(value, *others):
    return lax.optimization_barrier((value, *others))[0]


COLUMN = (0, 1, 3, 2)
NEAR, FAR = (0, -1, 1, -2, 2), (-3, 3, 4)


def attend(place, all_grad, near, far, near_other, far_other, queries, keys, values, attn, stats):
    parts, rows, depth = all_grad.shape
    width, key_width = queries.shape[1], keys.shape[1]
    return pl.pallas_call(
        attend_kernel,
        out_shape=(
            jax.ShapeDtypeStruct((rows, width), jnp.bfloat16),
            jax.ShapeDtypeStruct((rows, key_width), jnp.bfloat16),
            jax.ShapeDtypeStruct((rows, key_width), jnp.bfloat16),
        ),
        in_specs=[SMEM] + [HBM] * 10,
        out_specs=(VMEM, VMEM, VMEM),
        scratch_shapes=[
            pltpu.VMEM((X, 2, rows, depth), jnp.bfloat16),
            pltpu.VMEM((Z, X, 2, *near.shape[2:]), jnp.bfloat16),
            pltpu.VMEM(queries.shape, jnp.bfloat16),
            pltpu.VMEM(keys.shape, jnp.bfloat16),
            pltpu.VMEM(values.shape, jnp.bfloat16),
            pltpu.VMEM(attn.shape, jnp.bfloat16),
            pltpu.VMEM(stats.shape, jnp.float32),
            pltpu.VMEM((rows, width), jnp.float32),
            pltpu.VMEM((GROUP, rows, rows), jnp.float32),
            pltpu.VMEM((rows, width), jnp.bfloat16),
            pltpu.SemaphoreType.DMA((X, 2)),
            pltpu.SemaphoreType.DMA((2, 2 * Z)),
            pltpu.SemaphoreType.DMA((5,)),
        ],
        compiler_params=pltpu.CompilerParams(vmem_limit_bytes=60 << 20),
        cost_estimate=pl.CostEstimate(flops=4 << 30, bytes_accessed=12 << 20, transcendentals=1 << 20),
        name="attend",
    )(place, all_grad, near, far, near_other, far_other, queries, keys, values, attn, stats)


def on_device(
    queries, keys, values, attn_out, grad_out, out_weight, log_norm, source_row, dest_row, slot_start
):
    rows, width = queries.shape
    key_width = keys.shape[1]
    all_grad = lax.all_gather(grad_out, "tensor", axis=0, tiled=False)

    me = lax.axis_index("dp").astype(jnp.int32)
    first = (me * rows).reshape(1)
    place = jnp.stack([me // (2 * Z), (me // 2) % Z, me % 2])
    message = jax.ShapeDtypeStruct((HALO, width + 128), jnp.bfloat16)
    to_low, to_high, stats = pl.pallas_call(
        send_kernel,
        out_shape=(message, message, jax.ShapeDtypeStruct((128, rows), jnp.bfloat16)),
        in_specs=[SMEM] + [VMEM] * 4,
        out_specs=(VMEM,) * 3,
        scratch_shapes=[pltpu.VMEM((128, rows), jnp.float32)],
        cost_estimate=pl.CostEstimate(flops=2 * 2 * HALO * rows * 640, bytes_accessed=1 << 20, transcendentals=0),
        name="send_rows",
    )(first, source_row[None], slot_start[None], log_norm, attn_out)

    up = lambda x, z, c: (x, z + 1, c)
    down = lambda x, z, c: (x, z - 1, c)
    other = lambda x, z, c: (x, z, 1 - c)
    pair = jnp.concatenate([out_weight, move(out_weight, lambda x, z, c: (x ^ 1, z, c))], axis=0)
    column = jnp.concatenate([pair, move(pair, lambda x, z, c: (3 - x, z, c))], axis=0)
    column = after(column, to_low, to_high)
    up1, down1 = move(column, up), move(column, down)
    up2, down2 = move(up1, up), move(down1, down)
    up3 = move(up2, up)
    near = jnp.concatenate([column, up1, down1, up2, down2], axis=0)
    near_other = move(near, other)
    down3 = move(down2, down)
    up4 = move(up3, up)
    to_low, to_high = lax.optimization_barrier((to_low, to_high, down3))[:2]
    forward = [(i, i + 1) for i in range(lax.axis_size("dp") - 1)]
    from_low = lax.ppermute(to_high, "dp", forward)
    from_high = lax.ppermute(to_low, "dp", [(b, a) for a, b in forward])
    attn_packed, stats_packed = pl.pallas_call(
        receive_kernel,
        out_shape=(
            jax.ShapeDtypeStruct((rows, width), jnp.bfloat16),
            jax.ShapeDtypeStruct((16, rows), jnp.float32),
        ),
        in_specs=[SMEM] + [VMEM] * 5,
        out_specs=(VMEM, VMEM),
        cost_estimate=pl.CostEstimate(flops=2 * rows * rows * 640, bytes_accessed=2 << 20, transcendentals=0),
        name="receive_rows",
    )(first, dest_row[None], attn_out, stats, from_low, from_high)
    far = jnp.concatenate([up3, after(down3, attn_packed, stats_packed), up4], axis=0)
    far_other = move(after(far, all_grad), other)
    pieces = [piece.reshape(-1, X, *out_weight.shape) for piece in (near, far, near_other, far_other)]

    return attend(place, all_grad, *pieces, queries, keys, values, attn_packed, stats_packed)


def solution(mesh):
    in_specs = (P("dp", "tensor"),) * 6 + (P("tensor", "dp"), P("dp"), P("dp"), P("dp"))
    out_specs = (P("dp", "tensor"),) * 3
    return jax.shard_map(
        on_device, mesh=mesh, in_specs=in_specs, out_specs=out_specs, check_vma=False
    )
```
